32 devices in a mesh: groups: 2 (over x), tensor: 8 (over z, y), store: 2 (over core).
Axes of the slice: x: 2, y: 2, z: 4, core: 2. Of those that a mesh axis runs over, the one named last changes fastest.
Arguments:
- activations: bfloat16 [8192, 28672], P(('groups', 'store'), 'tensor'), parts along dimension 0, may hold values from -6 to 6
- out_grads: bfloat16 [8192, 8192], P(('groups', 'store', 'tensor')), parts along dimension 0, may hold values from -6 to 6
- factor_in: bfloat16 [28672, 64], P('tensor'), may hold values from -0.03125 to 0.03125
- factor_out: bfloat16 [8192, 64], replicated, may hold values from -0.0625 to 0.0625
- store_rows: bfloat16 [49152, 4096], P(('groups', 'tensor', 'store')), parts along dimension 0, may hold values from -0.09375 to 0.09375
Outputs:
- scores: float32 [32, 24576], P('groups', ('tensor', 'store')), parts along dimension 0
The draws below stay inside these ranges and needn't reach their ends.
There are 2 independent parts, one for each index of `groups`. The reference program is written for one: setup_inputs(seed, part) draws one part's arguments, and reference() takes and returns one part's arrays. A program takes and returns all parts, laid end to end along the dimension named above; an argument that names none is the same for every part. Nothing has to cross between parts.
All inputs are finite; a program needn't handle non-finite values.
Results may differ from the reference program's by a relative error of at most 0.0095.
Values may be sent and summed in bfloat16 or wider, within the bound.
A program may use at most 128 MiB of HBM per device.

```python
import jax
import jax.numpy as jnp
from jax import lax

IN_WIDTH = 28672
OUT_WIDTH = 8192
RANK = 64
SKETCH_WIDTH = 4096
UTT_LEN = 256
TOKENS = 4096
STORE_ROWS = 24576


def block_levels(rng, shape, pieces, smallest, top_value):
    factor_of = 1.0
    for dim, shards_of in pieces:
        heights = jax.random.uniform(jax.random.fold_in(jax.random.fold_in(rng, 6), dim), (shards_of,), jnp.float32, smallest / len(pieces), top_value / len(pieces))
        factor_of = factor_of * jnp.repeat(jnp.exp(heights), shape[dim] // shards_of).reshape((-1,) + (1,) * (len(shape) - 1 - dim))
    return factor_of


def scatter_about(own_key, dims, scale, most, shards=(), kind=jnp.bfloat16):
    entries = jax.random.normal(own_key, dims, jnp.float32) * scale
    if len(shards) > 0:
        entries = block_levels(own_key, dims, shards, -0.22, 0.18) * entries
    return jnp.clip(entries, min=-most, max=most).astype(kind)


def setup_inputs(seed: int = 0, part: int = 0) -> dict:
    splits = jax.random.split(jax.random.key(seed), 6)
    part_splits = jax.random.split(jax.random.fold_in(splits[5], part), 6)
    return {
        "activations": scatter_about(part_splits[0], (TOKENS, IN_WIDTH), 1.0, 6.0, ((0, 2), (1, 8))),
        "out_grads": scatter_about(part_splits[1], (TOKENS, OUT_WIDTH), 1.0, 6.0, ((0, 16),)),
        "factor_in": scatter_about(splits[2], (IN_WIDTH, RANK), IN_WIDTH ** -0.5, 0.03125, ((0, 8),)),
        "factor_out": scatter_about(splits[3], (OUT_WIDTH, RANK), OUT_WIDTH ** -0.5, 0.0625),
        "store_rows": scatter_about(part_splits[4], (STORE_ROWS, SKETCH_WIDTH), SKETCH_WIDTH ** -0.5, 0.09375, ((0, 16),)),
    }


def reference(activations, out_grads, factor_in, factor_out, store_rows):
    proj_in = jnp.dot(activations, factor_in, preferred_element_type=jnp.float32)
    proj_out = jnp.dot(out_grads, factor_out, preferred_element_type=jnp.float32)
    count = proj_in.shape[0] // UTT_LEN
    proj_in = proj_in.reshape(count, UTT_LEN, RANK)
    proj_out = proj_out.reshape(count, UTT_LEN, RANK)
    sketch = jnp.einsum('qta,qtb->qab', proj_out, proj_in) * (1.0 / jnp.sqrt(jnp.float32(UTT_LEN)))
    sketch = sketch.reshape(count, RANK * RANK).astype(jnp.bfloat16)
    return lax.dot_general(sketch, store_rows, (((1,), (1,)), ((), ())), preferred_element_type=jnp.float32)
```

```python
import functools

import jax
import jax.numpy as jnp
from jax import lax
from jax.experimental import pallas as pl
from jax.experimental.pallas import tpu as pltpu
from jax.sharding import PartitionSpec as P

RANK = 64
UTT_LEN = 256
PACK = 128 // RANK
STORE_CHUNKS = 4
GRAD_CHUNKS = 2
FORWARD_AFTER = 4
MESH = pl.DeviceIdType.MESH
NT = (((1,), (1,)), ((), ()))


def dot_nt(a, b):
    return lax.dot_general(a, b, NT, preferred_element_type=jnp.float32)


def kernel(
    T, S,
    act, grads, fin, fout, rows, out,
    act_v, grads_v, fin_v, fout_v, rows_v, proj_v, outer_v, part_v, send_v, recv_v, every_v, wide_v, sk_v, tmp_v,
    act_sem, grads_sem, fin_sem, fout_sem, rows_sem,
    g_send, g_recv, r_send, r_recv, e_send, e_recv,
):
    t = lax.axis_index("tensor")
    s = lax.axis_index("store")
    tokens = act.shape[0]
    count = tokens // UTT_LEN
    block = grads.shape[0]
    own = count * RANK // T
    packed = own // PACK
    lo, hi = lax.rem(t, 2), t // 2

    width = grads.shape[1] // GRAD_CHUNKS
    loads_g = []
    for c in range(GRAD_CHUNKS):
        cols = pl.ds(c * width, width)
        loads_g.append((
            pltpu.make_async_copy(fout.at[:, cols], fout_v.at[:, cols], fout_sem.at[c]),
            pltpu.make_async_copy(grads.at[:, cols], grads_v.at[:, cols], grads_sem.at[c]),
        ))
    for a, b in loads_g:
        a.start()
        b.start()
    loads_f = [
        pltpu.make_async_copy(fin, fin_v.at[pl.ds(i * RANK, RANK), :], fin_sem.at[i]) for i in range(PACK)
    ]
    for c in loads_f:
        c.start()

    def act_copy(q):
        r = pl.ds(pl.multiple_of(q * UTT_LEN, UTT_LEN), UTT_LEN)
        return pltpu.make_async_copy(act.at[r, :], act_v.at[r, :], act_sem.at[q])

    for q in range(count):
        act_copy(q).start()
    chunk = rows.shape[0] // STORE_CHUNKS

    def rows_copy(c):
        r = pl.ds(c * chunk, chunk)
        return pltpu.make_async_copy(rows.at[r, :], rows_v.at[r, :], rows_sem.at[c])

    for c in range(STORE_CHUNKS):
        rows_copy(c).start()

    barrier = pltpu.get_barrier_semaphore()
    peers = []
    for k in range(1, T):
        peers.append((lax.rem(t + k, T), s))
    for d in range(1, S):
        for k in range(T):
            peers.append((lax.rem(t + k, T), lax.rem(s + d, S)))
    for pt, ps in peers:
        pl.semaphore_signal(barrier, inc=1, device_id={"tensor": pt, "store": ps}, device_id_type=MESH)

    total = None
    for c, (a, b) in enumerate(loads_g):
        cols = pl.ds(c * width, width)
        a.wait()
        b.wait()
        term = dot_nt(fout_v[:, cols], grads_v[:, cols])
        total = term if total is None else total + term
    outer_v[t] = total.astype(jnp.bfloat16)
    pl.semaphore_wait(barrier, len(peers))

    def gather_copy(slot, to, n):
        return pltpu.make_async_remote_copy(
            src_ref=outer_v.at[slot], dst_ref=outer_v.at[slot],
            send_sem=g_send.at[n], recv_sem=g_recv.at[slot],
            device_id={"tensor": to}, device_id_type=MESH,
        )

    partner = hi * 2 + (1 - lo)
    half = T // 2
    sends = []
    for k in range(1, half):
        sends.append(gather_copy(t, lax.rem(hi + k, half) * 2 + lo, len(sends)))
    sends.append(gather_copy(t, partner, len(sends)))
    for c in sends:
        c.start()

    for c in loads_f:
        c.wait()

    def project(q, _):
        act_copy(q).wait()
        r = pl.ds(pl.multiple_of(q * UTT_LEN, UTT_LEN), UTT_LEN)
        proj_v[r, :] = dot_nt(act_v[r, :], fin_v[...]).astype(jnp.bfloat16)
        return 0

    lax.fori_loop(0, FORWARD_AFTER, project, 0)
    for k in range(1, half):
        slot = lax.rem(hi + k, half) * 2 + lo
        c = gather_copy(slot, partner, len(sends))
        c.wait_recv()
        c.start()
        sends.append(c)
    lax.fori_loop(FORWARD_AFTER, count, project, 0)
    for k in range(half):
        gather_copy(lax.rem(hi + k, half) * 2 + (1 - lo), partner, 0).wait_recv()

    blocks = UTT_LEN // block
    per_utt = RANK // own
    lane = lax.broadcasted_iota(jnp.int32, (packed, PACK * RANK), 1)

    def partial(owner):
        q = owner // per_utt
        a0 = pl.multiple_of(lax.rem(owner, per_utt) * own, own)
        acc = None
        for i in range(blocks):
            left = outer_v[q * blocks + i, pl.ds(a0, own), :]
            right = proj_v[pl.ds(pl.multiple_of((q * blocks + i) * block, block), block), :]
            term = jnp.dot(left, right, preferred_element_type=jnp.float32)
            acc = term if acc is None else acc + term
        part_v[...] = acc
        even = part_v[pl.ds(0, packed, stride=2), :]
        odd = part_v[pl.ds(1, packed, stride=2), :]
        return jnp.where(lane < RANK, even, odd)

    reduce_copies = []
    for k in range(1, T):
        to = lax.rem(t + k, T)
        send_v[to] = partial(to).astype(jnp.bfloat16)
        c = pltpu.make_async_remote_copy(
            src_ref=send_v.at[to], dst_ref=recv_v.at[t],
            send_sem=r_send.at[to], recv_sem=r_recv.at[t],
            device_id={"tensor": to}, device_id_type=MESH,
        )
        c.start()
        reduce_copies.append(c)
    tmp_v[...] = partial(t)
    for k in range(1, T):
        src = lax.rem(t + k, T)
        pltpu.make_async_remote_copy(
            src_ref=send_v.at[src], dst_ref=recv_v.at[src],
            send_sem=r_send.at[src], recv_sem=r_recv.at[src],
            device_id={"tensor": src}, device_id_type=MESH,
        ).wait_recv()
        tmp_v[...] += recv_v[src].astype(jnp.float32)
    me = s * T + t
    every_v[me] = (tmp_v[...] * (1.0 / UTT_LEN ** 0.5)).astype(jnp.bfloat16)

    def every_copy(pt, ps, slot):
        return pltpu.make_async_remote_copy(
            src_ref=every_v.at[slot], dst_ref=every_v.at[slot],
            send_sem=e_send.at[ps * T + pt], recv_sem=e_recv.at[slot],
            device_id={"tensor": pt, "store": ps}, device_id_type=MESH,
        )

    every_sends = [every_copy(pt, ps, me) for pt, ps in peers]
    for c in every_sends:
        c.start()
    for pt, ps in peers:
        every_copy(pt, ps, ps * T + pt).wait_recv()
    wide_v[...] = every_v[...].reshape(S * T * packed, PACK * RANK).astype(jnp.float32)
    lines = RANK // PACK
    for j in range(lines):
        sk_v[:, pl.ds(j * PACK * RANK, PACK * RANK)] = wide_v[
            pl.ds(j, S * count, stride=lines), :
        ].astype(jnp.bfloat16)
    for c in range(STORE_CHUNKS):
        rows_copy(c).wait()
        r = pl.ds(c * chunk, chunk)
        out[:, r] = dot_nt(rows_v[r, :], sk_v[...]).T

    for c in sends + reduce_copies + every_sends:
        c.wait_send()


def solution(mesh):
    T, S = mesh.shape["tensor"], mesh.shape["store"]

    def shards(activations, out_grads, factor_in, factor_out, store_rows):
        tokens, width = activations.shape
        block, out_width = out_grads.shape
        n_rows, sketch = store_rows.shape
        count = tokens // UTT_LEN
        own = count * RANK // T
        packed = own // PACK
        lanes = PACK * RANK
        bf, f32 = jnp.bfloat16, jnp.float32
        dma = pltpu.SemaphoreType.DMA
        flops = 2 * RANK * (tokens * width + block * out_width) + 2 * S * count * n_rows * sketch
        moved = 2 * (activations.size + out_grads.size + store_rows.size)
        return pl.pallas_call(
            functools.partial(kernel, T, S),
            out_shape=jax.ShapeDtypeStruct((S * count, n_rows), f32),
            in_specs=[pl.BlockSpec(memory_space=pl.ANY)] * 5,
            out_specs=pl.BlockSpec(memory_space=pltpu.VMEM),
            scratch_shapes=[
                pltpu.VMEM((tokens, width), bf),
                pltpu.VMEM((block, out_width), bf),
                pltpu.VMEM((lanes, width), bf),
                pltpu.VMEM((RANK, out_width), bf),
                pltpu.VMEM((n_rows, sketch), bf),
                pltpu.VMEM((tokens, lanes), bf),
                pltpu.VMEM((T, RANK, block), bf),
                pltpu.VMEM((own, lanes), f32),
                pltpu.VMEM((T, packed, lanes), bf),
                pltpu.VMEM((T, packed, lanes), bf),
                pltpu.VMEM((S * T, packed, lanes), bf),
                pltpu.VMEM((S * T * packed, lanes), f32),
                pltpu.VMEM((S * count, sketch), bf),
                pltpu.VMEM((packed, lanes), f32),
                dma((count,)), dma((GRAD_CHUNKS,)), dma((PACK,)), dma((GRAD_CHUNKS,)), dma((STORE_CHUNKS,)),
                dma((T,)), dma((T,)), dma((T,)), dma((T,)), dma((S * T,)), dma((S * T,)),
            ],
            compiler_params=pltpu.CompilerParams(
                collective_id=0, has_side_effects=True, vmem_limit_bytes=63 * 2**20
            ),
            cost_estimate=pl.CostEstimate(flops=flops, bytes_accessed=moved, transcendentals=0),
            name="sketch_scores",
        )(activations, out_grads, factor_in.T, factor_out.T, store_rows)

    in_specs = (
        P(("groups", "store"), "tensor"),
        P(("groups", "store", "tensor"), None),
        P("tensor", None),
        P(),
        P(("groups", "tensor", "store"), None),
    )
    out_specs = P("groups", ("tensor", "store"))
    return jax.shard_map(shards, mesh=mesh, in_specs=in_specs, out_specs=out_specs, check_vma=False)
```

```python
import functools

import jax
import jax.numpy as jnp
from jax import lax
from jax.experimental import pallas as pl
from jax.experimental.pallas import tpu as pltpu
from jax.sharding import PartitionSpec as P

RANK = 64
UTT_LEN = 256
PACK = 128 // RANK
STORE_CHUNKS = 4
GRAD_CHUNKS = 2
MESH = pl.DeviceIdType.MESH
NT = (((1,), (1,)), ((), ()))


def dot_nt(a, b):
    return lax.dot_general(a, b, NT, preferred_element_type=jnp.float32)


def kernel(
    T, S,
    act, grads, fin, fout, rows, out,
    act_v, grads_v, fin_v, fout_v, rows_v, proj_v, outer_v, part_v, send_v, recv_v, every_v, wide_v, sk_v,
    act_sem, grads_sem, fin_sem, fout_sem, rows_sem,
    g_send, g_recv, r_send, r_recv, e_send, e_recv,
):
    t = lax.axis_index("tensor")
    s = lax.axis_index("store")
    tokens = act.shape[0]
    count = tokens // UTT_LEN
    block = grads.shape[0]
    own = count * RANK // T
    packed = own // PACK

    width = grads.shape[1] // GRAD_CHUNKS
    loads_g = []
    for c in range(GRAD_CHUNKS):
        cols = pl.ds(c * width, width)
        loads_g.append((
            pltpu.make_async_copy(fout.at[:, cols], fout_v.at[:, cols], fout_sem.at[c]),
            pltpu.make_async_copy(grads.at[:, cols], grads_v.at[:, cols], grads_sem.at[c]),
        ))
    for a, b in loads_g:
        a.start()
        b.start()
    loads_f = [
        pltpu.make_async_copy(fin, fin_v.at[pl.ds(i * RANK, RANK), :], fin_sem.at[i]) for i in range(PACK)
    ]
    for c in loads_f:
        c.start()

    def act_copy(q):
        r = pl.ds(pl.multiple_of(q * UTT_LEN, UTT_LEN), UTT_LEN)
        return pltpu.make_async_copy(act.at[r, :], act_v.at[r, :], act_sem.at[q])

    for q in range(count):
        act_copy(q).start()
    chunk = rows.shape[0] // STORE_CHUNKS

    def rows_copy(c):
        r = pl.ds(c * chunk, chunk)
        return pltpu.make_async_copy(rows.at[r, :], rows_v.at[r, :], rows_sem.at[c])

    barrier = pltpu.get_barrier_semaphore()
    peers = []
    for k in range(1, T):
        peers.append((lax.rem(t + k, T), s))
    for d in range(1, S):
        for k in range(T):
            peers.append((lax.rem(t + k, T), lax.rem(s + d, S)))
    for pt, ps in peers:
        pl.semaphore_signal(barrier, inc=1, device_id={"tensor": pt, "store": ps}, device_id_type=MESH)

    total = None
    for c, (a, b) in enumerate(loads_g):
        cols = pl.ds(c * width, width)
        a.wait()
        b.wait()
        term = dot_nt(fout_v[:, cols], grads_v[:, cols])
        total = term if total is None else total + term
    outer_v[t] = total.astype(jnp.bfloat16)
    pl.semaphore_wait(barrier, len(peers))

    def gather_copy(slot, to, n):
        return pltpu.make_async_remote_copy(
            src_ref=outer_v.at[slot], dst_ref=outer_v.at[slot],
            send_sem=g_send.at[n], recv_sem=g_recv.at[slot],
            device_id={"tensor": to}, device_id_type=MESH,
        )

    sends = []
    for k in range(1, T):
        sends.append(gather_copy(t, lax.rem(t + k, T), len(sends)))
    for c in sends:
        c.start()

    for c in loads_f:
        c.wait()

    def project(q, _):
        act_copy(q).wait()
        r = pl.ds(pl.multiple_of(q * UTT_LEN, UTT_LEN), UTT_LEN)
        proj_v[r, :] = dot_nt(act_v[r, :], fin_v[...]).astype(jnp.bfloat16)
        return 0

    lax.fori_loop(0, count // 2, project, 0)
    for c in range(STORE_CHUNKS):
        rows_copy(c).start()
    lax.fori_loop(count // 2, count, project, 0)
    for k in range(1, T):
        gather_copy(lax.rem(t + k, T), t, 0).wait_recv()

    blocks = UTT_LEN // block
    per_utt = RANK // own
    lane = lax.broadcasted_iota(jnp.int32, (packed, PACK * RANK), 1)

    def reduce_copy(to, src):
        return pltpu.make_async_remote_copy(
            src_ref=send_v.at[to], dst_ref=recv_v.at[src],
            send_sem=r_send.at[to], recv_sem=r_recv.at[src],
            device_id={"tensor": to}, device_id_type=MESH,
        )

    def partial(q, _):
        for i in range(per_utt):
            owner = q * per_utt + i
            acc = None
            for n in range(blocks):
                left = outer_v[q * blocks + n, pl.ds(i * own, own), :]
                right = proj_v[pl.ds(pl.multiple_of((q * blocks + n) * block, block), block), :]
                term = jnp.dot(left, right, preferred_element_type=jnp.float32)
                acc = term if acc is None else acc + term
            part_v[...] = acc
            even = part_v[pl.ds(0, packed, stride=2), :]
            odd = part_v[pl.ds(1, packed, stride=2), :]
            mine = jnp.where(lane < RANK, even, odd).astype(jnp.bfloat16)

            @pl.when(owner != t)
            def _():
                send_v[owner] = mine
                reduce_copy(owner, t).start()

            @pl.when(owner == t)
            def _():
                recv_v[t] = mine
        return 0

    lax.fori_loop(0, count, partial, 0)

    for k in range(1, T):
        src = lax.rem(t + k, T)
        reduce_copy(src, src).wait_recv()
    summed = jnp.sum(recv_v[...].astype(jnp.float32), axis=0)
    me = s * T + t
    every_v[me] = (summed * (1.0 / UTT_LEN ** 0.5)).astype(jnp.bfloat16)

    def every_copy(pt, ps, slot):
        return pltpu.make_async_remote_copy(
            src_ref=every_v.at[slot], dst_ref=every_v.at[slot],
            send_sem=e_send.at[ps * T + pt], recv_sem=e_recv.at[slot],
            device_id={"tensor": pt, "store": ps}, device_id_type=MESH,
        )

    every_sends = [every_copy(pt, ps, me) for pt, ps in peers]
    for c in every_sends:
        c.start()
    for pt, ps in peers:
        every_copy(pt, ps, ps * T + pt).wait_recv()
    wide_v[...] = every_v[...].reshape(S * T * packed, PACK * RANK).astype(jnp.float32)
    lines = RANK // PACK
    for j in range(lines):
        sk_v[:, pl.ds(j * PACK * RANK, PACK * RANK)] = wide_v[
            pl.ds(j, S * count, stride=lines), :
        ].astype(jnp.bfloat16)
    for c in range(STORE_CHUNKS):
        rows_copy(c).wait()
    out[...] = dot_nt(rows_v[...], sk_v[...]).T

    for k in range(1, T):
        reduce_copy(lax.rem(t + k, T), t).wait_send()
    for c in sends + every_sends:
        c.wait_send()


def solution(mesh):
    T, S = mesh.shape["tensor"], mesh.shape["store"]

    def shards(activations, out_grads, factor_in, factor_out, store_rows):
        tokens, width = activations.shape
        block, out_width = out_grads.shape
        n_rows, sketch = store_rows.shape
        count = tokens // UTT_LEN
        own = count * RANK // T
        packed = own // PACK
        lanes = PACK * RANK
        bf, f32 = jnp.bfloat16, jnp.float32
        dma = pltpu.SemaphoreType.DMA
        flops = 2 * RANK * (tokens * width + block * out_width) + 2 * S * count * n_rows * sketch
        moved = 2 * (activations.size + out_grads.size + store_rows.size)
        return pl.pallas_call(
            functools.partial(kernel, T, S),
            out_shape=jax.ShapeDtypeStruct((S * count, n_rows), f32),
            in_specs=[pl.BlockSpec(memory_space=pl.ANY)] * 5,
            out_specs=pl.BlockSpec(memory_space=pltpu.VMEM),
            scratch_shapes=[
                pltpu.VMEM((tokens, width), bf),
                pltpu.VMEM((block, out_width), bf),
                pltpu.VMEM((lanes, width), bf),
                pltpu.VMEM((RANK, out_width), bf),
                pltpu.VMEM((n_rows, sketch), bf),
                pltpu.VMEM((tokens, lanes), bf),
                pltpu.VMEM((T, RANK, block), bf),
                pltpu.VMEM((own, lanes), f32),
                pltpu.VMEM((T, packed, lanes), bf),
                pltpu.VMEM((T, packed, lanes), bf),
                pltpu.VMEM((S * T, packed, lanes), bf),
                pltpu.VMEM((S * T * packed, lanes), f32),
                pltpu.VMEM((S * count, sketch), bf),
                dma((count,)), dma((GRAD_CHUNKS,)), dma((PACK,)), dma((GRAD_CHUNKS,)), dma((STORE_CHUNKS,)),
                dma((T,)), dma((T,)), dma((T,)), dma((T,)), dma((S * T,)), dma((S * T,)),
            ],
            compiler_params=pltpu.CompilerParams(
                collective_id=0, has_side_effects=True, vmem_limit_bytes=63 * 2**20
            ),
            cost_estimate=pl.CostEstimate(flops=flops, bytes_accessed=moved, transcendentals=0),
            name="sketch_scores",
        )(activations, out_grads, factor_in.T, factor_out.T, store_rows)

    in_specs = (
        P(("groups", "store"), "tensor"),
        P(("groups", "store", "tensor"), None),
        P("tensor", None),
        P(),
        P(("groups", "tensor", "store"), None),
    )
    out_specs = P("groups", ("tensor", "store"))
    return jax.shard_map(shards, mesh=mesh, in_specs=in_specs, out_specs=out_specs, check_vma=False)
```

```python
import functools

import jax
import jax.numpy as jnp
from jax import lax
from jax.experimental import pallas as pl
from jax.experimental.pallas import tpu as pltpu
from jax.sharding import PartitionSpec as P

RANK = 64
UTT_LEN = 256
PACK = 128 // RANK
STORE_CHUNKS = 4
GRAD_CHUNKS = 2
MESH = pl.DeviceIdType.MESH
NT = (((1,), (1,)), ((), ()))


def dot_nt(a, b):
    return lax.dot_general(a, b, NT, preferred_element_type=jnp.float32)


def kernel(
    T, S,
    act, grads, fin, fout, rows, out,
    act_v, grads_v, fin_v, fout_v, rows_v, proj_v, outer_v, part_v, send_v, recv_v, every_v, wide_v, sk_v,
    act_sem, grads_sem, fin_sem, fout_sem, rows_sem,
    g_send, g_recv, r_send, r_recv, e_send, e_recv,
):
    t = lax.axis_index("tensor")
    s = lax.axis_index("store")
    tokens = act.shape[0]
    count = tokens // UTT_LEN
    block = grads.shape[0]
    owners, first = T // 2, T // 4
    per = count // owners
    packed = RANK // PACK
    mine = t - first
    is_owner = (t >= first) & (t < first + owners)

    width = grads.shape[1] // GRAD_CHUNKS
    loads_g = []
    for c in range(GRAD_CHUNKS):
        cols = pl.ds(c * width, width)
        loads_g.append((
            pltpu.make_async_copy(fout.at[:, cols], fout_v.at[:, cols], fout_sem.at[c]),
            pltpu.make_async_copy(grads.at[:, cols], grads_v.at[:, cols], grads_sem.at[c]),
        ))
    for a, b in loads_g:
        a.start()
        b.start()
    loads_f = [
        pltpu.make_async_copy(fin, fin_v.at[pl.ds(i * RANK, RANK), :], fin_sem.at[i]) for i in range(PACK)
    ]
    for c in loads_f:
        c.start()

    def act_copy(q):
        r = pl.ds(pl.multiple_of(q * UTT_LEN, UTT_LEN), UTT_LEN)
        return pltpu.make_async_copy(act.at[r, :], act_v.at[r, :], act_sem.at[q])

    for q in range(count):
        act_copy(q).start()
    chunk = rows.shape[0] // STORE_CHUNKS

    def rows_copy(c):
        r = pl.ds(c * chunk, chunk)
        return pltpu.make_async_copy(rows.at[r, :], rows_v.at[r, :], rows_sem.at[c])

    barrier = pltpu.get_barrier_semaphore()
    peers = []
    for k in range(1, T):
        peers.append((lax.rem(t + k, T), s))
    for d in range(1, S):
        for k in range(T):
            peers.append((lax.rem(t + k, T), lax.rem(s + d, S)))
    for pt, ps in peers:
        pl.semaphore_signal(barrier, inc=1, device_id={"tensor": pt, "store": ps}, device_id_type=MESH)

    total = None
    for c, (a, b) in enumerate(loads_g):
        cols = pl.ds(c * width, width)
        a.wait()
        b.wait()
        term = dot_nt(fout_v[:, cols], grads_v[:, cols])
        total = term if total is None else total + term
    outer_v[t] = total.astype(jnp.bfloat16)
    pl.semaphore_wait(barrier, len(peers))

    def gather_copy(slot, to, n):
        return pltpu.make_async_remote_copy(
            src_ref=outer_v.at[slot], dst_ref=outer_v.at[slot],
            send_sem=g_send.at[n], recv_sem=g_recv.at[slot],
            device_id={"tensor": to}, device_id_type=MESH,
        )

    sends = []
    for k in range(1, T):
        sends.append(gather_copy(t, lax.rem(t + k, T), len(sends)))
    for c in sends:
        c.start()

    for c in loads_f:
        c.wait()

    def project(q, _):
        act_copy(q).wait()
        r = pl.ds(pl.multiple_of(q * UTT_LEN, UTT_LEN), UTT_LEN)
        proj_v[r, :] = dot_nt(act_v[r, :], fin_v[...]).astype(jnp.bfloat16)
        return 0

    lax.fori_loop(0, count // 2, project, 0)
    for c in range(STORE_CHUNKS):
        rows_copy(c).start()
    lax.fori_loop(count // 2, count, project, 0)
    for k in range(1, T):
        gather_copy(lax.rem(t + k, T), t, 0).wait_recv()

    blocks = UTT_LEN // block
    lane = lax.broadcasted_iota(jnp.int32, (packed, PACK * RANK), 1)

    def reduce_copy(q, src):
        return pltpu.make_async_remote_copy(
            src_ref=send_v.at[q], dst_ref=recv_v.at[lax.rem(q, per), src],
            send_sem=r_send.at[q], recv_sem=r_recv.at[lax.rem(q, per) * T + src],
            device_id={"tensor": first + q // per}, device_id_type=MESH,
        )

    def partial(q, _):
        acc = None
        for n in range(blocks):
            right = proj_v[pl.ds(pl.multiple_of((q * blocks + n) * block, block), block), :]
            term = jnp.dot(outer_v[q * blocks + n], right, preferred_element_type=jnp.float32)
            acc = term if acc is None else acc + term
        part_v[...] = acc
        even = part_v[pl.ds(0, packed, stride=2), :]
        odd = part_v[pl.ds(1, packed, stride=2), :]
        value = jnp.where(lane < RANK, even, odd).astype(jnp.bfloat16)
        home = first + q // per

        @pl.when(home != t)
        def _():
            send_v[q] = value
            reduce_copy(q, t).start()

        @pl.when(home == t)
        def _():
            recv_v[lax.rem(q, per), t] = value
        return 0

    lax.fori_loop(0, count, partial, 0)

    def every_copy(pt, ps, o, os):
        slots = pl.ds(os * count + o * per, per)
        return pltpu.make_async_remote_copy(
            src_ref=every_v.at[slots], dst_ref=every_v.at[slots],
            send_sem=e_send.at[ps * T + pt], recv_sem=e_recv.at[os * owners + o],
            device_id={"tensor": pt, "store": ps}, device_id_type=MESH,
        )

    @pl.when(is_owner)
    def _():
        for j in range(per):
            for k in range(1, T):
                reduce_copy(j, lax.rem(t + k, T)).wait_recv()
        for j in range(per):
            summed = jnp.sum(recv_v[j].astype(jnp.float32), axis=0)
            every_v[s * count + mine * per + j] = (summed * (1.0 / UTT_LEN ** 0.5)).astype(jnp.bfloat16)
        for pt, ps in peers:
            every_copy(pt, ps, mine, s).start()

    for os in range(S):
        for o in range(owners):
            @pl.when((s != os) | (t != first + o))
            def _():
                every_copy(t, s, o, os).wait_recv()
    wide_v[...] = every_v[...].reshape(S * count * packed, PACK * RANK).astype(jnp.float32)
    lines = RANK // PACK
    for j in range(lines):
        sk_v[:, pl.ds(j * PACK * RANK, PACK * RANK)] = wide_v[
            pl.ds(j, S * count, stride=lines), :
        ].astype(jnp.bfloat16)
    for c in range(STORE_CHUNKS):
        rows_copy(c).wait()
    out[...] = dot_nt(rows_v[...], sk_v[...]).T

    for q in range(count):
        @pl.when(t != first + q // per)
        def _():
            reduce_copy(q, t).wait_send()

    @pl.when(is_owner)
    def _():
        for pt, ps in peers:
            every_copy(pt, ps, mine, s).wait_send()

    for c in sends:
        c.wait_send()


def solution(mesh):
    T, S = mesh.shape["tensor"], mesh.shape["store"]

    def shards(activations, out_grads, factor_in, factor_out, store_rows):
        tokens, width = activations.shape
        block, out_width = out_grads.shape
        n_rows, sketch = store_rows.shape
        count = tokens // UTT_LEN
        packed = RANK // PACK
        per = count // (T // 2)
        lanes = PACK * RANK
        bf, f32 = jnp.bfloat16, jnp.float32
        dma = pltpu.SemaphoreType.DMA
        flops = 2 * RANK * (tokens * width + block * out_width) + 2 * S * count * n_rows * sketch
        moved = 2 * (activations.size + out_grads.size + store_rows.size)
        return pl.pallas_call(
            functools.partial(kernel, T, S),
            out_shape=jax.ShapeDtypeStruct((S * count, n_rows), f32),
            in_specs=[pl.BlockSpec(memory_space=pl.ANY)] * 5,
            out_specs=pl.BlockSpec(memory_space=pltpu.VMEM),
            scratch_shapes=[
                pltpu.VMEM((tokens, width), bf),
                pltpu.VMEM((block, out_width), bf),
                pltpu.VMEM((lanes, width), bf),
                pltpu.VMEM((RANK, out_width), bf),
                pltpu.VMEM((n_rows, sketch), bf),
                pltpu.VMEM((tokens, lanes), bf),
                pltpu.VMEM((T, RANK, block), bf),
                pltpu.VMEM((RANK, lanes), f32),
                pltpu.VMEM((count, packed, lanes), bf),
                pltpu.VMEM((per, T, packed, lanes), bf),
                pltpu.VMEM((S * count, packed, lanes), bf),
                pltpu.VMEM((S * count * packed, lanes), f32),
                pltpu.VMEM((S * count, sketch), bf),
                dma((count,)), dma((GRAD_CHUNKS,)), dma((PACK,)), dma((GRAD_CHUNKS,)), dma((STORE_CHUNKS,)),
                dma((T,)), dma((T,)), dma((count,)), dma((per * T,)), dma((S * T,)), dma((S * T,)),
            ],
            compiler_params=pltpu.CompilerParams(
                collective_id=0, has_side_effects=True, vmem_limit_bytes=63 * 2**20
            ),
            cost_estimate=pl.CostEstimate(flops=flops, bytes_accessed=moved, transcendentals=0),
            name="sketch_scores",
        )(activations, out_grads, factor_in.T, factor_out.T, store_rows)

    in_specs = (
        P(("groups", "store"), "tensor"),
        P(("groups", "store", "tensor"), None),
        P("tensor", None),
        P(),
        P(("groups", "tensor", "store"), None),
    )
    out_specs = P("groups", ("tensor", "store"))
    return jax.shard_map(shards, mesh=mesh, in_specs=in_specs, out_specs=out_specs, check_vma=False)
```
